256 devices in a mesh: ctx: 32 (over z, y_lo, core), head: 8 (over y_hi, x).
Axes of the slice: x: 4, y: 4 (y_hi: 2, y_lo: 2; y = y_hi * 2 + y_lo), z: 8, core: 2. Of those that a mesh axis runs over, the one named last changes fastest.
Arguments:
- queries: bfloat16 [512, 8192], P(('ctx', 'head')), may hold values from -150 to 150
- keys: bfloat16 [131072, 1024], P('ctx', 'head'), may hold values from -4 to 4
- values: bfloat16 [131072, 1024], P('ctx', 'head'), may hold values from -6 to 6
- doc_len: int32 [8], replicated, may hold values from 32768 to 131072, as said below
Outputs:
- attended: bfloat16 [512, 8192], P('ctx', 'head')
The draws below stay inside these ranges and needn't reach their ends.
Inputs may be any that keep to these rules, and one draw needn't show every extreme that they name: Candidate c sees the first doc_len[c] document tokens; in every draw some candidate sees all 131072.
All inputs are finite; a program needn't handle non-finite values.
Results may differ from the reference program's by a relative error of at most 0.004.
Values may be sent and summed in bfloat16 or wider, within the bound.
No kernel may reach another device: no remote copies, remote signals or barrier semaphores. Data moves between devices by JAX's collectives and lax.ppermute only.
A program may use at most 64 MiB of HBM per device.

```python
import math
import jax
import jax.numpy as jnp
from jax import lax

HQ = 64
KVH = 8
HD = 128
QPK = 8
TILE = 512
NDOC = 131072
CANDS = 8
CAND_LEN = 64
ROWS = 512


def common_draw(key):
    key_base = jax.random.fold_in(key, 0)
    base_keys = jnp.clip(jax.random.normal(key_base, (NDOC, KVH, HD), jnp.float32), -4.0, 4.0)
    return base_keys


def draw_keys(key, part):
    base_keys = common_draw(key)
    return base_keys.reshape(NDOC, KVH * HD).astype(jnp.bfloat16)


def draw_queries(key, part):
    key = jax.random.fold_in(key, 2)
    drawn = jnp.clip(3.0 * jax.random.normal(key, (ROWS, KVH, QPK, HD), jnp.float32), -12.0, 12.0)
    return drawn.reshape(ROWS, HQ * HD).astype(jnp.bfloat16)


def draw_doc_len(key, part):
    key = jax.random.fold_in(key, 3)
    key_len, key_selection = jax.random.split(key)
    lengths = jax.random.randint(key_len, (CANDS,), NDOC // 4, NDOC + 1)
    chosen = jax.random.randint(key_selection, (), 0, CANDS)
    return lengths.at[chosen].set(NDOC).astype(jnp.int32)


def steps_of(stream_key, dims, cuts, least, top_value):
    factor_of = 1.0
    for axis_at, parts in cuts:
        steps = jax.random.uniform(jax.random.fold_in(jax.random.fold_in(stream_key, 6), axis_at), (parts,), jnp.float32, least / len(cuts), top_value / len(cuts))
        factor_of = factor_of * jnp.repeat(jnp.exp(steps), dims[axis_at] // parts).reshape((-1,) + (1,) * (len(dims) - 1 - axis_at))
    return factor_of


def noise(rng, shape, scale, most, shards=(), kind=jnp.bfloat16):
    array = scale * jax.random.normal(rng, shape, jnp.float32)
    if shards:
        array = array * steps_of(rng, shape, shards, -0.22, 0.18)
    return jnp.clip(array, -most, most).astype(kind)


def setup_inputs(seed: int = 0) -> dict:
    streams_of = jax.random.split(jax.random.key(seed), 5)
    queries = draw_queries(jax.random.fold_in(streams_of[4], 71), 0)
    keys = draw_keys(jax.random.fold_in(streams_of[4], 71), 0)
    values = noise(streams_of[2], (NDOC, KVH * HD), 1.0, 6.0, ((0, 32), (1, 8)))
    doc_len = draw_doc_len(jax.random.fold_in(streams_of[4], 71), 0)
    return {"queries": queries, "keys": keys, "values": values, "doc_len": doc_len}


def reference(queries, keys, values, doc_len):
    score_scale = 1.0 / math.sqrt(HD)
    score_rows = ROWS * QPK
    grouped_q = queries.astype(jnp.float32).reshape(ROWS, KVH, QPK, HD).transpose(1, 0, 2, 3).reshape(KVH, score_rows, HD)
    grouped_k = keys.astype(jnp.float32).reshape(NDOC, KVH, HD).transpose(1, 0, 2)
    grouped_v = values.astype(jnp.float32).reshape(NDOC, KVH, HD).transpose(1, 0, 2)
    visible = jnp.repeat(doc_len, CAND_LEN * QPK)
    block_len = math.gcd(NDOC, 8192)
    tile_count = block_len // TILE
    starts = jnp.arange(NDOC // block_len, dtype=jnp.int32) * block_len

    def one_group(operands):
        query_rows, key_rows, value_rows = operands

        def block_advance(carry, start):
            running, totals, numerators = carry
            key_tile = lax.dynamic_slice_in_dim(key_rows, start, block_len, 0)
            logits = jnp.dot(query_rows, key_tile.T, precision=lax.Precision.HIGHEST) * score_scale
            positions = start + jnp.arange(block_len, dtype=jnp.int32)
            usable = positions[None, :] < visible[:, None]
            logits = logits.reshape(score_rows, tile_count, TILE)
            usable = usable.reshape(score_rows, tile_count, TILE)
            tile_top = lax.optimization_barrier(jnp.max(jnp.where(usable, logits, -1e+30), axis=2))
            weights = jnp.where(usable, jnp.exp(logits - tile_top[:, :, None]), 0.0)
            rounded_length = lax.optimization_barrier(weights.astype(jnp.bfloat16)).astype(jnp.float32)
            value_slab = lax.dynamic_slice_in_dim(value_rows, start, block_len, 0).reshape(tile_count, TILE, HD)
            tile_position = jnp.einsum('wcx,cxj->wcj', rounded_length, value_slab, precision=lax.Precision.HIGHEST)
            tile_sum = lax.optimization_barrier(jnp.sum(weights, axis=2))
            new_top = jnp.maximum(running, lax.optimization_barrier(jnp.max(tile_top, axis=1)))
            old_scale = jnp.exp(running - new_top)
            fresh = jnp.exp(tile_top - new_top[:, None])
            totals = old_scale * totals + lax.optimization_barrier(jnp.sum(fresh * tile_sum, axis=1))
            numerators = old_scale[:, None] * numerators + lax.optimization_barrier(jnp.sum(fresh[:, :, None] * tile_position, axis=1))
            return ((new_top, totals, numerators), None)
        start_carry = (jnp.full((score_rows,), -1e+30, jnp.float32), jnp.zeros((score_rows,), jnp.float32), jnp.zeros((score_rows, HD), jnp.float32))
        (running, totals, numerators), _ = lax.scan(block_advance, start_carry, starts)
        return (numerators / totals[:, None]).astype(jnp.bfloat16)
    attended = lax.map(one_group, (grouped_q, grouped_k, grouped_v))
    return attended.reshape(KVH, ROWS, QPK, HD).transpose(1, 0, 2, 3).reshape(ROWS, HQ * HD)
```

```python
import functools

import jax
import jax.numpy as jnp
from jax import lax
from jax.experimental import pallas as pl
from jax.experimental.pallas import tpu as pltpu
from jax.sharding import Mesh
from jax.sharding import PartitionSpec as P

HD = 128
QPK = 8
CANDS = 8
HALF = 4096
LANES = 512
CAND_LANES = 256
GROUPS = CANDS * CAND_LANES // LANES
SAMPLE = 128
EXTRA = 16
NONE = -1e30
LIMIT = 2.0**60
LOG2_SCALE = 1.4426950408889634 / HD**0.5
NT = (((1,), (1,)), ((), ()))


def scores(key_rows, query_rows):
    s = lax.dot_general(key_rows, query_rows, NT, preferred_element_type=jnp.float32)
    return s * LOG2_SCALE


def attend_kernel(
    info, q_ref, k_own, k_other, vt_own, vt_other, out_ref, top_ref, acc_ref, sum_ref, big_ref
):
    base_own, base_other = info[CANDS], info[CANDS + 1]
    base = jnp.minimum(base_own, base_other)
    lane = lax.broadcasted_iota(jnp.int32, (1, LANES), 1)

    def visible(group):
        first = info[group * 2]
        second = info[group * 2 + 1]
        return jnp.where(lane < CAND_LANES, first, second)

    def group_queries(group):
        return q_ref[pl.ds(pl.multiple_of(group * LANES, LANES), LANES), :]

    def store(group, numerators, total, top):
        total_high = total.astype(jnp.bfloat16).astype(jnp.float32)
        row = lax.broadcasted_iota(jnp.int32, (EXTRA, LANES), 0)
        extra = jnp.where(row == 0, top, 0.0)
        extra = jnp.where(row == 1, total_high, extra)
        extra = jnp.where(row == 2, total - total_high, extra)
        for j in range(LANES // HD):
            cut = slice(j * HD, (j + 1) * HD)
            out_ref[group * (LANES // HD) + j, :HD, :] = numerators[:, cut].astype(jnp.bfloat16)
            out_ref[group * (LANES // HD) + j, HD:, :] = extra[:, cut].astype(jnp.bfloat16)

    first_keys = jnp.where(base_own == base, k_own[:SAMPLE, :], k_other[:SAMPLE, :])
    place = base + lax.broadcasted_iota(jnp.int32, (SAMPLE, LANES), 0)
    for group in range(GROUPS):
        s = scores(first_keys, q_ref[group * LANES : (group + 1) * LANES, :])
        top = jnp.max(jnp.where(place < visible(group), s, NONE), axis=0, keepdims=True)
        top_ref[group] = top.astype(jnp.bfloat16).astype(jnp.float32)
    big_ref[...] = jnp.zeros_like(big_ref)

    @pl.loop(0, GROUPS)
    def _(group):
        query_rows = group_queries(group)
        top = top_ref[group]
        least = jnp.minimum(info[group * 2], info[group * 2 + 1])
        most = jnp.maximum(info[group * 2], info[group * 2 + 1])
        full = least >= base + 2 * HALF

        @pl.when(full)
        def _():
            total = jnp.zeros((8, LANES), jnp.float32)
            numerators = jnp.zeros((HD, LANES), jnp.float32)
            for k_ref, vt_ref in ((k_own, vt_own), (k_other, vt_other)):
                weights = jnp.exp2(scores(k_ref[...], query_rows) - top)
                total += jnp.sum(weights.reshape(HALF // 8, 8, LANES), axis=0)
                numerators += jnp.dot(
                    vt_ref[...], weights.astype(jnp.bfloat16), preferred_element_type=jnp.float32
                )
            total = jnp.sum(total, axis=0, keepdims=True)
            big_ref[...] = jnp.maximum(big_ref[...], total)
            store(group, numerators, total, top)

        @pl.when(jnp.logical_not(full))
        def _():
            block = 1024
            acc_ref[...] = jnp.zeros_like(acc_ref)
            sum_ref[...] = jnp.zeros_like(sum_ref)
            seen = visible(group)
            for k_ref, vt_ref, start in (
                (k_own, vt_own, base_own),
                (k_other, vt_other, base_other),
            ):
                count = (jnp.clip(most - start, 0, HALF) + block - 1) // block

                @pl.loop(0, count)
                def _(i):
                    at = pl.multiple_of(i * block, block)
                    place = start + at + lax.broadcasted_iota(jnp.int32, (block, LANES), 0)
                    weights = jnp.exp2(scores(k_ref[pl.ds(at, block), :], query_rows) - top)
                    weights = jnp.where(place < seen, weights, 0.0)
                    sum_ref[...] += jnp.sum(weights.reshape(block // 8, 8, LANES), axis=0)
                    acc_ref[...] += jnp.dot(
                        vt_ref[:, pl.ds(at, block)],
                        weights.astype(jnp.bfloat16),
                        preferred_element_type=jnp.float32,
                    )

            total = jnp.sum(sum_ref[...], axis=0, keepdims=True)
            big_ref[...] = jnp.maximum(big_ref[...], total)
            store(group, acc_ref[...], total, top)

    @pl.when(jnp.logical_not(jnp.max(big_ref[...]) < LIMIT))
    def _():
        block = 512

        @pl.loop(0, GROUPS)
        def _(group):
            query_rows = group_queries(group)
            seen = visible(group)
            acc_ref[...] = jnp.zeros_like(acc_ref)
            sum_ref[...] = jnp.zeros_like(sum_ref)
            top_ref[group] = jnp.full((1, LANES), NONE, jnp.float32)
            for k_ref, vt_ref, start in (
                (k_own, vt_own, base_own),
                (k_other, vt_other, base_other),
            ):

                @pl.loop(0, HALF // block)
                def _(i):
                    at = pl.multiple_of(i * block, block)
                    place = start + at + lax.broadcasted_iota(jnp.int32, (block, LANES), 0)
                    usable = place < seen
                    s = jnp.where(usable, scores(k_ref[pl.ds(at, block), :], query_rows), NONE)
                    old = top_ref[group]
                    new = jnp.maximum(old, jnp.max(s, axis=0, keepdims=True))
                    shrink = jnp.exp2(old - new)
                    weights = jnp.where(usable, jnp.exp2(s - new), 0.0)
                    sum_ref[...] = sum_ref[...] * shrink + jnp.sum(
                        weights.reshape(block // 8, 8, LANES), axis=0
                    )
                    acc_ref[...] = acc_ref[...] * shrink + jnp.dot(
                        vt_ref[:, pl.ds(at, block)],
                        weights.astype(jnp.bfloat16),
                        preferred_element_type=jnp.float32,
                    )
                    top_ref[group] = new

            top = top_ref[group]
            sent = top.astype(jnp.bfloat16).astype(jnp.float32)
            fit = jnp.where(top > 0.5 * NONE, jnp.exp2(top - sent), 1.0)
            total = jnp.sum(sum_ref[...], axis=0, keepdims=True)
            store(group, acc_ref[...] * fit, total * fit, sent)


def combine_kernel(x_ref, out_ref, turned_ref):
    parts = x_ref.shape[0]
    tops = [x_ref[i, HD:, :].astype(jnp.float32)[0:1] for i in range(parts)]
    top = functools.reduce(jnp.maximum, tops)
    total = jnp.zeros((1, HD), jnp.float32)
    numerators = jnp.zeros((HD, HD), jnp.float32)
    for i in range(parts):
        scale = jnp.exp2(tops[i] - top)
        extra = x_ref[i, HD:, :].astype(jnp.float32)
        total += scale * (extra[1:2] + extra[2:3])
        numerators += scale * x_ref[i, :HD, :].astype(jnp.float32)
    turned_ref[...] = (numerators / total).T
    for h in range(QPK):
        rows = turned_ref[pl.ds(h, HD // QPK, stride=QPK), :]
        out_ref[:, h * HD : (h + 1) * HD] = rows.astype(jnp.bfloat16)


def attend(info, q, k_own, k_other, vt_own, vt_other):
    in_vmem = pl.BlockSpec(memory_space=pltpu.VMEM)
    pieces = q.shape[0] // HD
    work = q.shape[0] * 2 * HALF
    return pl.pallas_call(
        attend_kernel,
        out_shape=jax.ShapeDtypeStruct((pieces, HD + EXTRA, HD), jnp.bfloat16),
        in_specs=[pl.BlockSpec(memory_space=pltpu.SMEM)] + [in_vmem] * 5,
        out_specs=in_vmem,
        scratch_shapes=[
            pltpu.VMEM((GROUPS, 1, LANES), jnp.float32),
            pltpu.VMEM((HD, LANES), jnp.float32),
            pltpu.VMEM((8, LANES), jnp.float32),
            pltpu.VMEM((1, LANES), jnp.float32),
        ],
        compiler_params=pltpu.CompilerParams(vmem_limit_bytes=52 * 2**20),
        cost_estimate=pl.CostEstimate(
            flops=4 * work * HD, bytes_accessed=6 * 2**20, transcendentals=work
        ),
        name="attend",
    )(info, q, k_own, k_other, vt_own, vt_other)


def combine(x):
    in_vmem = pl.BlockSpec(memory_space=pltpu.VMEM)
    return pl.pallas_call(
        combine_kernel,
        out_shape=jax.ShapeDtypeStruct((HD // QPK, QPK * HD), jnp.bfloat16),
        in_specs=[in_vmem],
        out_specs=in_vmem,
        scratch_shapes=[pltpu.VMEM((HD, HD), jnp.float32)],
        cost_estimate=pl.CostEstimate(
            flops=4 * x.size, bytes_accessed=2 * x.size, transcendentals=0
        ),
        name="combine",
    )(x)


def body(queries, keys, values, doc_len):
    swap = [(0, 1), (1, 0)]
    k_other = lax.ppermute(keys, "c", swap)
    vt_own = values.T
    vt_other = lax.ppermute(vt_own, "c", swap)

    rows = queries.shape[0]
    heads = lax.axis_size(("h", "x"))
    spans = lax.axis_size(("z", "y"))
    blocks = queries.reshape(rows, heads, QPK, HD).transpose(1, 0, 2, 3)
    blocks = blocks.reshape(1, heads, rows * QPK, HD)
    blocks = jnp.broadcast_to(blocks, (spans, heads, rows * QPK, HD))
    q = lax.all_to_all(
        blocks.reshape(spans * heads, rows * QPK, HD), ("z", "y", "h", "x"), 0, 0
    ).reshape(spans * heads * rows * QPK, HD)

    chip = lax.axis_index(("z", "y")) * (2 * HALF)
    core = lax.axis_index("c")
    info = jnp.concatenate(
        [doc_len, jnp.stack([chip + core * HALF, chip + (1 - core) * HALF]).astype(jnp.int32)]
    )
    partial = attend(info, q, keys, k_other, vt_own, vt_other)
    return combine(lax.all_to_all(partial, ("z", "y"), 0, 0))


def solution(mesh):
    fine = Mesh(mesh.devices.reshape(8, 2, 2, 2, 4), ("z", "y", "c", "h", "x"))
    ctx, head = ("z", "y", "c"), ("h", "x")
    placed = (P(ctx + head, None), P(ctx, head), P(ctx, head), P())
    return jax.shard_map(
        body, mesh=fine, in_specs=placed, out_specs=P(ctx, head), check_vma=False
    )
```

```python
import functools

import jax
import jax.numpy as jnp
from jax import lax
from jax.experimental import pallas as pl
from jax.experimental.pallas import tpu as pltpu
from jax.sharding import Mesh
from jax.sharding import PartitionSpec as P

HD = 128
QPK = 8
CANDS = 8
HALF = 4096
LANES = 512
CAND_LANES = 128
MEMBERS = LANES // CAND_LANES
GROUPS = CANDS // MEMBERS
SAMPLE = 128
EXTRA = 16
NONE = -1e30
LIMIT = 2.0**60
LOG2_SCALE = 1.4426950408889634 / HD**0.5
NT = (((1,), (1,)), ((), ()))
TN = (((0,), (0,)), ((), ()))


def scores(key_rows, query_rows):
    s = lax.dot_general(key_rows, query_rows, NT, preferred_element_type=jnp.float32)
    return s * LOG2_SCALE


def weighted(value_rows, weights):
    return lax.dot_general(
        value_rows, weights.astype(jnp.bfloat16), TN, preferred_element_type=jnp.float32
    )


def attend_kernel(
    info, q_ref, k_own, k_other, v_own, v_other, out_ref, top_ref, acc_ref, sum_ref, big_ref
):
    base_own, base_other, part = info[CANDS], info[CANDS + 1], info[CANDS + 2]
    base = jnp.minimum(base_own, base_other)
    end = base + 2 * HALF
    halves = ((k_own, v_own, base_own), (k_other, v_other, base_other))
    lane = lax.broadcasted_iota(jnp.int32, (1, LANES), 1)

    def visible(group):
        seen = info[group * MEMBERS]
        for j in range(1, MEMBERS):
            seen = jnp.where(lane < j * CAND_LANES, seen, info[group * MEMBERS + j])
        return seen

    def group_queries(group):
        rows = [q_ref[group * MEMBERS + j, part] for j in range(MEMBERS)]
        return jnp.concatenate(rows, axis=0)

    def store(group, numerators, total, top):
        extra = split_total(total, top, LANES)
        for j in range(MEMBERS):
            cut = slice(j * HD, (j + 1) * HD)
            out_ref[group * MEMBERS + j, :HD, :] = numerators[:, cut].astype(jnp.bfloat16)
            out_ref[group * MEMBERS + j, HD:, :] = extra[:, cut]

    first_keys = jnp.where(base_own == base, k_own[:SAMPLE, :], k_other[:SAMPLE, :])
    place = base + lax.broadcasted_iota(jnp.int32, (SAMPLE, LANES), 0)
    for group in range(GROUPS):
        s = scores(first_keys, group_queries(group))
        top = jnp.max(jnp.where(place < visible(group), s, NONE), axis=0, keepdims=True)
        top_ref[group] = top.astype(jnp.bfloat16).astype(jnp.float32)
    big_ref[...] = jnp.zeros_like(big_ref)

    def one_pass(group, masked):
        query_rows = group_queries(group)
        top = top_ref[group]
        point = jnp.where(top > 0.5 * NONE, top, -NONE)
        seen = visible(group)
        total = jnp.zeros((8, LANES), jnp.float32)
        numerators = jnp.zeros((HD, LANES), jnp.float32)
        for k_ref, v_ref, start in halves:
            weights = jnp.exp2(scores(k_ref[...], query_rows) - point)
            if masked:
                place = start + lax.broadcasted_iota(jnp.int32, (HALF, LANES), 0)
                weights = jnp.where(place < seen, weights, 0.0)
            total += jnp.sum(weights.reshape(HALF // 8, 8, LANES), axis=0)
            numerators += weighted(v_ref[...], weights)
        total = jnp.sum(total, axis=0, keepdims=True)
        big_ref[...] = jnp.maximum(big_ref[...], total)
        store(group, numerators, total, top)

    @pl.loop(0, GROUPS)
    def _(group):
        lengths = [info[group * MEMBERS + j] for j in range(MEMBERS)]
        idle = functools.reduce(jnp.maximum, lengths) <= base
        whole = functools.reduce(
            jnp.logical_and, [jnp.logical_or(n <= base, n >= end) for n in lengths]
        )
        plain = jnp.logical_and(whole, jnp.logical_not(idle))
        mixed = jnp.logical_not(whole)

        @pl.when(idle)
        def _():
            nothing = jnp.zeros((1, LANES), jnp.float32)
            store(group, jnp.zeros((HD, LANES), jnp.float32), nothing, nothing + NONE)

        @pl.when(plain)
        def _():
            one_pass(group, False)

        @pl.when(mixed)
        def _():
            one_pass(group, True)

    @pl.when(jnp.logical_not(jnp.max(big_ref[...]) < LIMIT))
    def _():
        block = 512

        @pl.loop(0, GROUPS)
        def _(group):
            query_rows = group_queries(group)
            seen = visible(group)
            acc_ref[...] = jnp.zeros_like(acc_ref)
            sum_ref[...] = jnp.zeros_like(sum_ref)
            top_ref[group] = jnp.full((1, LANES), NONE, jnp.float32)
            for k_ref, v_ref, start in halves:

                @pl.loop(0, HALF // block)
                def _(i):
                    at = pl.multiple_of(i * block, block)
                    place = start + at + lax.broadcasted_iota(jnp.int32, (block, LANES), 0)
                    usable = place < seen
                    s = jnp.where(usable, scores(k_ref[pl.ds(at, block), :], query_rows), NONE)
                    old = top_ref[group]
                    new = jnp.maximum(old, jnp.max(s, axis=0, keepdims=True))
                    shrink = jnp.exp2(old - new)
                    weights = jnp.where(usable, jnp.exp2(s - new), 0.0)
                    sum_ref[...] = sum_ref[...] * shrink + jnp.sum(
                        weights.reshape(block // 8, 8, LANES), axis=0
                    )
                    acc_ref[...] = acc_ref[...] * shrink + weighted(
                        v_ref[pl.ds(at, block), :], weights
                    )
                    top_ref[group] = new

            top = top_ref[group]
            sent = top.astype(jnp.bfloat16).astype(jnp.float32)
            fit = jnp.where(top > 0.5 * NONE, jnp.exp2(top - sent), 1.0)
            total = jnp.sum(sum_ref[...], axis=0, keepdims=True)
            store(group, acc_ref[...] * fit, total * fit, sent)


def split_total(total, top, width):
    total_high = total.astype(jnp.bfloat16).astype(jnp.float32)
    row = lax.broadcasted_iota(jnp.int32, (EXTRA, width), 0)
    extra = jnp.where(row == 0, top, 0.0)
    extra = jnp.where(row == 1, total_high, extra)
    return jnp.where(row == 2, total - total_high, extra).astype(jnp.bfloat16)


def summed(pieces):
    extras = [piece[HD:, :].astype(jnp.float32) for piece in pieces]
    top = functools.reduce(jnp.maximum, [extra[0:1] for extra in extras])
    total = jnp.zeros((1, HD), jnp.float32)
    numerators = jnp.zeros((HD, HD), jnp.float32)
    for piece, extra in zip(pieces, extras, strict=True):
        scale = jnp.exp2(extra[0:1] - top)
        total += scale * (extra[1:2] + extra[2:3])
        numerators += scale * piece[:HD, :].astype(jnp.float32)
    return numerators, total, top


def merge_kernel(a_ref, b_ref, out_ref):
    for i in range(out_ref.shape[0]):
        numerators, total, top = summed([a_ref[i], b_ref[i]])
        out_ref[i, :HD, :] = numerators.astype(jnp.bfloat16)
        out_ref[i, HD:, :] = split_total(total, top, HD)


def combine_kernel(x_ref, out_ref, turned_ref):
    numerators, total, _ = summed([x_ref[i] for i in range(x_ref.shape[0])])
    turned_ref[...] = (numerators / total).T
    for h in range(QPK):
        rows = turned_ref[pl.ds(h, HD // QPK, stride=QPK), :]
        out_ref[:, h * HD : (h + 1) * HD] = rows.astype(jnp.bfloat16)


def attend(info, q, k_own, k_other, v_own, v_other):
    in_vmem = pl.BlockSpec(memory_space=pltpu.VMEM)
    work = q.size // HD // 2 * 2 * HALF
    return pl.pallas_call(
        attend_kernel,
        out_shape=jax.ShapeDtypeStruct((CANDS, HD + EXTRA, HD), jnp.bfloat16),
        in_specs=[pl.BlockSpec(memory_space=pltpu.SMEM)] + [in_vmem] * 5,
        out_specs=in_vmem,
        scratch_shapes=[
            pltpu.VMEM((GROUPS, 1, LANES), jnp.float32),
            pltpu.VMEM((HD, LANES), jnp.float32),
            pltpu.VMEM((8, LANES), jnp.float32),
            pltpu.VMEM((1, LANES), jnp.float32),
        ],
        compiler_params=pltpu.CompilerParams(vmem_limit_bytes=32 * 2**20),
        cost_estimate=pl.CostEstimate(
            flops=4 * work * HD, bytes_accessed=6 * 2**20, transcendentals=work
        ),
        name="attend",
    )(info, q, k_own, k_other, v_own, v_other)


def merge(a, b):
    in_vmem = pl.BlockSpec(memory_space=pltpu.VMEM)
    return pl.pallas_call(
        merge_kernel,
        out_shape=jax.ShapeDtypeStruct(a.shape, jnp.bfloat16),
        in_specs=[in_vmem] * 2,
        out_specs=in_vmem,
        compiler_params=pltpu.CompilerParams(vmem_limit_bytes=8 * 2**20),
        cost_estimate=pl.CostEstimate(
            flops=8 * a.size, bytes_accessed=6 * a.size, transcendentals=0
        ),
        name="merge",
    )(a, b)


def combine(x):
    in_vmem = pl.BlockSpec(memory_space=pltpu.VMEM)
    return pl.pallas_call(
        combine_kernel,
        out_shape=jax.ShapeDtypeStruct((HD // QPK, QPK * HD), jnp.bfloat16),
        in_specs=[in_vmem],
        out_specs=in_vmem,
        scratch_shapes=[pltpu.VMEM((HD, HD), jnp.float32)],
        compiler_params=pltpu.CompilerParams(vmem_limit_bytes=8 * 2**20),
        cost_estimate=pl.CostEstimate(
            flops=4 * x.size, bytes_accessed=2 * x.size, transcendentals=0
        ),
        name="combine",
    )(x)


def body(queries, keys, values, doc_len):
    swap = [(0, 1), (1, 0)]
    k_other = lax.ppermute(keys, "c", swap)
    v_other = lax.ppermute(values, "c", swap)

    rows = queries.shape[0]
    heads = lax.axis_size(("h", "x"))
    spans = lax.axis_size(("z", "y"))
    blocks = queries.reshape(rows, heads, QPK, HD).transpose(1, 0, 2, 3)
    blocks = blocks.reshape(1, heads, rows * QPK, HD)
    blocks = jnp.broadcast_to(blocks, (spans, heads, rows * QPK, HD))
    q = lax.all_to_all(
        blocks.reshape(spans * heads, rows * QPK, HD), ("z", "y", "h", "x"), 0, 0
    ).reshape(CANDS, spans // CANDS, heads * rows * QPK, HD)

    chip = lax.axis_index(("z", "y")) * (2 * HALF)
    core, side = lax.axis_index("c"), lax.axis_index("y")
    bases = [chip + core * HALF, chip + (1 - core) * HALF]

    def info(part):
        return jnp.concatenate([doc_len, jnp.stack(bases + [part]).astype(jnp.int32)])

    foreign = attend(info(1 - side), q, keys, k_other, values, v_other)
    received = lax.ppermute(foreign, "y", swap)
    own = attend(info(side), q, keys, k_other, values, v_other)
    return combine(lax.all_to_all(merge(own, received), "z", 0, 0))


def solution(mesh):
    fine = Mesh(mesh.devices.reshape(8, 2, 2, 2, 4), ("z", "y", "c", "h", "x"))
    ctx, head = ("z", "y", "c"), ("h", "x")
    placed = (P(ctx + head, None), P(ctx, head), P(ctx, head), P())
    return jax.shard_map(
        body, mesh=fine, in_specs=placed, out_specs=P(ctx, head), check_vma=False
    )
```

```python
import functools

import jax
import jax.numpy as jnp
from jax import lax
from jax.experimental import pallas as pl
from jax.experimental.pallas import tpu as pltpu
from jax.sharding import Mesh
from jax.sharding import PartitionSpec as P

HD = 128
QPK = 8
CANDS = 8
HALF = 4096
LANES = 1024
CAND_LANES = 128
MEMBERS = LANES // CAND_LANES
GROUPS = CANDS // MEMBERS
SAMPLE = 128
EXTRA = 16
NONE = -1e30
HIDDEN = -(2.0**100)
LIMIT = 2.0**60
LOG2_SCALE = 1.4426950408889634 / HD**0.5
NT = (((1,), (1,)), ((), ()))
TN = (((0,), (0,)), ((), ()))


def scores(key_rows, query_rows):
    s = lax.dot_general(key_rows, query_rows, NT, preferred_element_type=jnp.float32)
    return s * LOG2_SCALE


def weighted(value_rows, weights):
    return lax.dot_general(
        value_rows, weights.astype(jnp.bfloat16), TN, preferred_element_type=jnp.float32
    )


def block_kernel(q_ref, out_ref, rows_ref):
    rows, heads = q_ref.shape[0], q_ref.shape[1] // (QPK * HD)
    q = q_ref[...].astype(jnp.float32)
    for g in range(heads):
        for i in range(rows):
            for h in range(QPK):
                at = (g * rows + i) * QPK + h
                cut = slice((g * QPK + h) * HD, (g * QPK + h + 1) * HD)
                rows_ref[at : at + 1, :] = q[i : i + 1, cut]
    blocks = rows_ref[...].astype(jnp.bfloat16).reshape(heads, rows * QPK, HD)
    for j in range(out_ref.shape[0]):
        out_ref[j] = blocks


def attend_kernel(info, q_ref, k_ref, v_ref, out_ref, top_ref, acc_ref, sum_ref, big_ref):
    base_own, base_other, part = info[CANDS], info[CANDS + 1], info[CANDS + 2]
    base = jnp.minimum(base_own, base_other)
    halves = ((0, base_own), (HALF, base_other))
    lane = lax.broadcasted_iota(jnp.int32, (1, LANES), 1)

    def visible(group):
        seen = info[group * MEMBERS]
        for j in range(1, MEMBERS):
            seen = jnp.where(lane < j * CAND_LANES, seen, info[group * MEMBERS + j])
        return seen

    def group_queries(group):
        rows = [q_ref[group * MEMBERS + j, part] for j in range(MEMBERS)]
        return jnp.concatenate(rows, axis=0)

    def store(group, numerators, total, top):
        extra = split_total(total, top, LANES)
        for j in range(MEMBERS):
            cut = slice(j * HD, (j + 1) * HD)
            out_ref[group * MEMBERS + j, :HD, :] = numerators[:, cut].astype(out_ref.dtype)
            out_ref[group * MEMBERS + j, HD:, :] = extra[:, cut].astype(out_ref.dtype)

    first = pl.multiple_of(jnp.where(base_own == base, 0, HALF), HALF)
    first_keys = k_ref[pl.ds(first, SAMPLE), :]
    place = base + lax.broadcasted_iota(jnp.int32, (SAMPLE, LANES), 0)
    for group in range(GROUPS):
        s = scores(first_keys, group_queries(group))
        top = jnp.max(jnp.where(place < visible(group), s, NONE), axis=0, keepdims=True)
        top_ref[group] = top.astype(jnp.bfloat16).astype(jnp.float32)
    big_ref[...] = jnp.zeros_like(big_ref)

    @pl.loop(0, GROUPS)
    def _(group):
        lengths = [info[group * MEMBERS + j] for j in range(MEMBERS)]
        idle = functools.reduce(jnp.maximum, lengths) <= base

        @pl.when(idle)
        def _():
            nothing = jnp.zeros((1, LANES), jnp.float32)
            store(group, jnp.zeros((HD, LANES), jnp.float32), nothing, nothing + NONE)

        @pl.when(jnp.logical_not(idle))
        def _():
            column = lax.broadcasted_iota(jnp.int32, (1, HD), 1)
            limit = functools.reduce(
                lambda rest, j: jnp.where(column == j, lengths[j], rest),
                range(MEMBERS),
                jnp.full((1, HD), 2**30, jnp.int32),
            )
            member = lax.broadcasted_iota(jnp.int32, (LANES, HD), 0) // CAND_LANES
            column = lax.broadcasted_iota(jnp.int32, (LANES, HD), 1)
            veto = jnp.where(member == column, HIDDEN, 0.0).astype(jnp.bfloat16)
            query_rows = jnp.concatenate([group_queries(group), veto], axis=1)
            top = top_ref[group]
            point = jnp.where(top > 0.5 * NONE, top, -NONE)
            total = jnp.zeros((8, LANES), jnp.float32)
            numerators = jnp.zeros((HD, LANES), jnp.float32)
            for half, start in halves:
                place = start + lax.broadcasted_iota(jnp.int32, (HALF, HD), 0)
                unseen = jnp.where(place >= limit, 1.0, 0.0).astype(jnp.bfloat16)
                key_rows = jnp.concatenate([k_ref[half : half + HALF, :], unseen], axis=1)
                weights = jnp.exp2(scores(key_rows, query_rows) - point)
                total += jnp.sum(weights.reshape(HALF // 8, 8, LANES), axis=0)
                numerators += weighted(v_ref[half : half + HALF, :], weights)
            total = jnp.sum(total, axis=0, keepdims=True)
            big_ref[...] = jnp.maximum(big_ref[...], total)
            store(group, numerators, total, top)

    @pl.when(jnp.logical_not(jnp.max(big_ref[...]) < LIMIT))
    def _():
        block = 512

        @pl.loop(0, GROUPS)
        def _(group):
            query_rows = group_queries(group)
            seen = visible(group)
            acc_ref[...] = jnp.zeros_like(acc_ref)
            sum_ref[...] = jnp.zeros_like(sum_ref)
            top_ref[group] = jnp.full((1, LANES), NONE, jnp.float32)
            for half, start in halves:

                @pl.loop(0, HALF // block)
                def _(i):
                    at = pl.multiple_of(half + i * block, block)
                    place = start + i * block + lax.broadcasted_iota(jnp.int32, (block, LANES), 0)
                    usable = place < seen
                    s = jnp.where(usable, scores(k_ref[pl.ds(at, block), :], query_rows), NONE)
                    old = top_ref[group]
                    new = jnp.maximum(old, jnp.max(s, axis=0, keepdims=True))
                    shrink = jnp.exp2(old - new)
                    weights = jnp.where(usable, jnp.exp2(s - new), 0.0)
                    sum_ref[...] = sum_ref[...] * shrink + jnp.sum(
                        weights.reshape(block // 8, 8, LANES), axis=0
                    )
                    acc_ref[...] = acc_ref[...] * shrink + weighted(
                        v_ref[pl.ds(at, block), :], weights
                    )
                    top_ref[group] = new

            top = top_ref[group]
            sent = top.astype(jnp.bfloat16).astype(jnp.float32)
            fit = jnp.where(top > 0.5 * NONE, jnp.exp2(top - sent), 1.0)
            total = jnp.sum(sum_ref[...], axis=0, keepdims=True)
            store(group, acc_ref[...] * fit, total * fit, sent)


def split_total(total, top, width):
    total_high = total.astype(jnp.bfloat16).astype(jnp.float32)
    row = lax.broadcasted_iota(jnp.int32, (EXTRA, width), 0)
    extra = jnp.where(row == 0, top, 0.0)
    extra = jnp.where(row == 1, total_high, extra)
    return jnp.where(row == 2, total - total_high, extra).astype(jnp.bfloat16)


def summed(pieces):
    extras = [piece[HD:, :].astype(jnp.float32) for piece in pieces]
    top = functools.reduce(jnp.maximum, [extra[0:1] for extra in extras])
    total = jnp.zeros((1, HD), jnp.float32)
    numerators = jnp.zeros((HD, HD), jnp.float32)
    for piece, extra in zip(pieces, extras, strict=True):
        scale = jnp.exp2(extra[0:1] - top)
        total += scale * (extra[1:2] + extra[2:3])
        numerators += scale * piece[:HD, :].astype(jnp.float32)
    return numerators, total, top


def merge_kernel(a_ref, b_ref, out_ref):
    for i in range(out_ref.shape[0]):
        numerators, total, top = summed([a_ref[i], b_ref[i]])
        out_ref[i, :HD, :] = numerators.astype(jnp.bfloat16)
        out_ref[i, HD:, :] = split_total(total, top, HD)


def combine_kernel(x_ref, out_ref, turned_ref):
    numerators, total, _ = summed([x_ref[i] for i in range(x_ref.shape[0])])
    turned_ref[...] = (numerators / total).T
    for h in range(QPK):
        rows = turned_ref[pl.ds(h, HD // QPK, stride=QPK), :]
        out_ref[:, h * HD : (h + 1) * HD] = rows.astype(jnp.bfloat16)


def build_blocks(queries, heads, spans):
    in_vmem = pl.BlockSpec(memory_space=pltpu.VMEM)
    rows = queries.shape[0] * QPK
    return pl.pallas_call(
        block_kernel,
        out_shape=jax.ShapeDtypeStruct((spans, heads, rows, HD), jnp.bfloat16),
        in_specs=[in_vmem],
        out_specs=in_vmem,
        scratch_shapes=[pltpu.VMEM((heads * rows, HD), jnp.float32)],
        compiler_params=pltpu.CompilerParams(vmem_limit_bytes=8 * 2**20),
        cost_estimate=pl.CostEstimate(
            flops=0, bytes_accessed=2 * spans * queries.size, transcendentals=0
        ),
        name="build_blocks",
    )(queries)


def attend(info, q, k, v, dtype):
    in_vmem = pl.BlockSpec(memory_space=pltpu.VMEM)
    work = q.size // HD // 2 * 2 * HALF
    return pl.pallas_call(
        attend_kernel,
        out_shape=jax.ShapeDtypeStruct((CANDS, HD + EXTRA, HD), dtype),
        in_specs=[pl.BlockSpec(memory_space=pltpu.SMEM)] + [in_vmem] * 3,
        out_specs=in_vmem,
        scratch_shapes=[
            pltpu.VMEM((GROUPS, 1, LANES), jnp.float32),
            pltpu.VMEM((HD, LANES), jnp.float32),
            pltpu.VMEM((8, LANES), jnp.float32),
            pltpu.VMEM((1, LANES), jnp.float32),
        ],
        compiler_params=pltpu.CompilerParams(vmem_limit_bytes=40 * 2**20),
        cost_estimate=pl.CostEstimate(
            flops=4 * work * HD, bytes_accessed=6 * 2**20, transcendentals=work
        ),
        name="attend",
    )(info, q, k, v)


def merge(a, b):
    in_vmem = pl.BlockSpec(memory_space=pltpu.VMEM)
    return pl.pallas_call(
        merge_kernel,
        out_shape=jax.ShapeDtypeStruct(a.shape, jnp.bfloat16),
        in_specs=[in_vmem] * 2,
        out_specs=in_vmem,
        compiler_params=pltpu.CompilerParams(vmem_limit_bytes=8 * 2**20),
        cost_estimate=pl.CostEstimate(
            flops=8 * a.size, bytes_accessed=6 * a.size, transcendentals=0
        ),
        name="merge",
    )(a, b)


def combine(x):
    in_vmem = pl.BlockSpec(memory_space=pltpu.VMEM)
    return pl.pallas_call(
        combine_kernel,
        out_shape=jax.ShapeDtypeStruct((HD // QPK, QPK * HD), jnp.bfloat16),
        in_specs=[in_vmem],
        out_specs=in_vmem,
        scratch_shapes=[pltpu.VMEM((HD, HD), jnp.float32)],
        compiler_params=pltpu.CompilerParams(vmem_limit_bytes=8 * 2**20),
        cost_estimate=pl.CostEstimate(
            flops=4 * x.size, bytes_accessed=2 * x.size, transcendentals=0
        ),
        name="combine",
    )(x)


def body(queries, keys, values, doc_len):
    swap = [(0, 1), (1, 0)]
    k = jnp.concatenate([keys, lax.ppermute(keys, "c", swap)], axis=0)
    v = jnp.concatenate([values, lax.ppermute(values, "c", swap)], axis=0)

    heads = lax.axis_size(("h", "x"))
    spans = lax.axis_size(("z", "y"))
    blocks = build_blocks(queries, heads, spans)
    q = lax.all_to_all(
        blocks.reshape((spans * heads,) + blocks.shape[2:]), ("z", "y", "h", "x"), 0, 0
    ).reshape(CANDS, spans // CANDS, CAND_LANES, HD)

    chip = lax.axis_index(("z", "y")) * (2 * HALF)
    core, side = lax.axis_index("c"), lax.axis_index("y")
    bases = [chip + core * HALF, chip + (1 - core) * HALF]

    def info(part):
        return jnp.concatenate([doc_len, jnp.stack(bases + [part]).astype(jnp.int32)])

    foreign = attend(info(1 - side), q, k, v, jnp.bfloat16)
    received = lax.ppermute(foreign, "y", swap)
    own = attend(info(side), q, k, v, jnp.float32)
    return combine(lax.all_to_all(merge(own, received), "z", 0, 0))


def solution(mesh):
    fine = Mesh(mesh.devices.reshape(8, 2, 2, 2, 4), ("z", "y", "c", "h", "x"))
    ctx, head = ("z", "y", "c"), ("h", "x")
    placed = (P(ctx + head, None), P(ctx, head), P(ctx, head), P())
    return jax.shard_map(
        body, mesh=fine, in_specs=placed, out_specs=P(ctx, head), check_vma=False
    )
```

```python
import functools

import jax
import jax.numpy as jnp
from jax import lax
from jax.experimental import pallas as pl
from jax.experimental.pallas import tpu as pltpu
from jax.sharding import Mesh
from jax.sharding import PartitionSpec as P

HD = 128
QPK = 8
CANDS = 8
HALF = 4096
CAND_LANES = 128
LANES = CANDS * CAND_LANES
SAMPLE = 128
EXTRA = 16
NONE = -1e30
HIDDEN = -(2.0**100)
LIMIT = 2.0**60
LOG2_SCALE = 1.4426950408889634 / HD**0.5
NT = (((1,), (1,)), ((), ()))
TN = (((0,), (0,)), ((), ()))


def scores(key_rows, query_rows):
    s = lax.dot_general(key_rows, query_rows, NT, preferred_element_type=jnp.float32)
    return s * LOG2_SCALE


def weighted(value_rows, weights):
    return lax.dot_general(
        value_rows, weights.astype(jnp.bfloat16), TN, preferred_element_type=jnp.float32
    )


def block_kernel(q_ref, out_ref, rows_ref):
    rows, heads = q_ref.shape[0], q_ref.shape[1] // (QPK * HD)
    q = q_ref[...].astype(jnp.float32)
    for g in range(heads):
        for i in range(rows):
            for h in range(QPK):
                at = (g * rows + i) * QPK + h
                cut = slice((g * QPK + h) * HD, (g * QPK + h + 1) * HD)
                rows_ref[at : at + 1, :] = q[i : i + 1, cut]
    blocks = rows_ref[...].astype(jnp.bfloat16).reshape(heads, rows * QPK, HD)
    for j in range(out_ref.shape[0]):
        out_ref[j] = blocks


def attend_kernel(info, q_ref, k_ref, v_ref, out_ref, top_ref, acc_ref, sum_ref):
    base_own, base_other, part = info[CANDS], info[CANDS + 1], info[CANDS + 2]
    base = jnp.minimum(base_own, base_other)
    halves = ((0, base_own), (HALF, base_other))
    lengths = [info[c] for c in range(CANDS)]

    def per_candidate(values, lane):
        result = values[0]
        for c in range(1, CANDS):
            result = jnp.where(lane < c * CAND_LANES, result, values[c])
        return result

    def store(first, count, numerators, total, top):
        extra = split_total(total, top, count * HD)
        for j in range(count):
            cut = slice(j * HD, (j + 1) * HD)
            out_ref[first + j, :HD, :] = numerators[:, cut].astype(out_ref.dtype)
            out_ref[first + j, HD:, :] = extra[:, cut].astype(out_ref.dtype)

    queries = jnp.concatenate([q_ref[c, part] for c in range(CANDS)], axis=0)

    first = pl.multiple_of(jnp.where(base_own == base, 0, HALF), HALF)
    place = base + lax.broadcasted_iota(jnp.int32, (SAMPLE, LANES), 0)
    seen = per_candidate(lengths, lax.broadcasted_iota(jnp.int32, (1, LANES), 1))
    top = jnp.where(place < seen, scores(k_ref[pl.ds(first, SAMPLE), :], queries), NONE)
    top = jnp.max(top, axis=0, keepdims=True).astype(jnp.bfloat16).astype(jnp.float32)
    point = jnp.where(top > 0.5 * NONE, top, -NONE)

    column = lax.broadcasted_iota(jnp.int32, (1, HD), 1)
    limit = jnp.full((1, HD), 2**30, jnp.int32)
    for c in range(CANDS):
        limit = jnp.where(column == c, lengths[c], limit)
    member = lax.broadcasted_iota(jnp.int32, (LANES, HD), 0) // CAND_LANES
    column = lax.broadcasted_iota(jnp.int32, (LANES, HD), 1)
    veto = jnp.where(member == column, HIDDEN, 0.0).astype(jnp.bfloat16)
    query_rows = jnp.concatenate([queries, veto], axis=1)

    total = jnp.zeros((8, LANES), jnp.float32)
    numerators = jnp.zeros((HD, LANES), jnp.float32)
    for half, start in halves:
        lead = (start + 1 - limit).astype(jnp.float32)
        row = lax.broadcasted_iota(jnp.int32, (HALF, HD), 0).astype(jnp.float32)
        beyond = jnp.maximum(row + lead, 0.0).astype(jnp.bfloat16)
        key_rows = jnp.concatenate([k_ref[half : half + HALF, :], beyond], axis=1)
        weights = jnp.exp2(scores(key_rows, query_rows) - point)
        total += jnp.sum(weights.reshape(HALF // 8, 8, LANES), axis=0)
        numerators += weighted(v_ref[half : half + HALF, :], weights)
    total = jnp.sum(total, axis=0, keepdims=True)
    store(0, CANDS, numerators, total, top)

    @pl.when(jnp.logical_not(jnp.max(total) < LIMIT))
    def _():
        block = 512

        @pl.loop(0, CANDS)
        def _(c):
            query_rows = q_ref[c, part]
            acc_ref[...] = jnp.zeros_like(acc_ref)
            sum_ref[...] = jnp.zeros_like(sum_ref)
            top_ref[...] = jnp.full_like(top_ref, NONE)
            for half, start in halves:

                @pl.loop(0, HALF // block)
                def _(i):
                    at = pl.multiple_of(half + i * block, block)
                    place = start + i * block + lax.broadcasted_iota(
                        jnp.int32, (block, CAND_LANES), 0
                    )
                    usable = place < info[c]
                    s = jnp.where(usable, scores(k_ref[pl.ds(at, block), :], query_rows), NONE)
                    old = top_ref[...]
                    new = jnp.maximum(old, jnp.max(s, axis=0, keepdims=True))
                    shrink = jnp.exp2(old - new)
                    weights = jnp.where(usable, jnp.exp2(s - new), 0.0)
                    sum_ref[...] = sum_ref[...] * shrink + jnp.sum(
                        weights.reshape(block // 8, 8, CAND_LANES), axis=0
                    )
                    acc_ref[...] = acc_ref[...] * shrink + weighted(
                        v_ref[pl.ds(at, block), :], weights
                    )
                    top_ref[...] = new

            top = top_ref[...]
            sent = top.astype(jnp.bfloat16).astype(jnp.float32)
            fit = jnp.where(top > 0.5 * NONE, jnp.exp2(top - sent), 1.0)
            total = jnp.sum(sum_ref[...], axis=0, keepdims=True)
            store(c, 1, acc_ref[...] * fit, total * fit, sent)


def split_total(total, top, width):
    total_high = total.astype(jnp.bfloat16).astype(jnp.float32)
    row = lax.broadcasted_iota(jnp.int32, (EXTRA, width), 0)
    extra = jnp.where(row == 0, top, 0.0)
    extra = jnp.where(row == 1, total_high, extra)
    return jnp.where(row == 2, total - total_high, extra).astype(jnp.bfloat16)


def summed(pieces):
    extras = [piece[HD:, :].astype(jnp.float32) for piece in pieces]
    top = functools.reduce(jnp.maximum, [extra[0:1] for extra in extras])
    total = jnp.zeros((1, HD), jnp.float32)
    numerators = jnp.zeros((HD, HD), jnp.float32)
    for piece, extra in zip(pieces, extras, strict=True):
        scale = jnp.exp2(extra[0:1] - top)
        total += scale * (extra[1:2] + extra[2:3])
        numerators += scale * piece[:HD, :].astype(jnp.float32)
    return numerators, total, top


def merge_kernel(a_ref, b_ref, out_ref):
    for i in range(out_ref.shape[0]):
        numerators, total, top = summed([a_ref[i], b_ref[i]])
        out_ref[i, :HD, :] = numerators.astype(jnp.bfloat16)
        out_ref[i, HD:, :] = split_total(total, top, HD)


def combine_kernel(x_ref, out_ref, turned_ref):
    numerators, total, _ = summed([x_ref[i] for i in range(x_ref.shape[0])])
    turned_ref[...] = (numerators / total).T
    for h in range(QPK):
        rows = turned_ref[pl.ds(h, HD // QPK, stride=QPK), :]
        out_ref[:, h * HD : (h + 1) * HD] = rows.astype(jnp.bfloat16)


def build_blocks(queries, heads, spans):
    in_vmem = pl.BlockSpec(memory_space=pltpu.VMEM)
    rows = queries.shape[0] * QPK
    return pl.pallas_call(
        block_kernel,
        out_shape=jax.ShapeDtypeStruct((spans, heads, rows, HD), jnp.bfloat16),
        in_specs=[in_vmem],
        out_specs=in_vmem,
        scratch_shapes=[pltpu.VMEM((heads * rows, HD), jnp.float32)],
        compiler_params=pltpu.CompilerParams(vmem_limit_bytes=8 * 2**20),
        cost_estimate=pl.CostEstimate(
            flops=0, bytes_accessed=2 * spans * queries.size, transcendentals=0
        ),
        name="build_blocks",
    )(queries)


def attend(info, q, k, v, dtype):
    in_vmem = pl.BlockSpec(memory_space=pltpu.VMEM)
    work = q.size // HD // 2 * 2 * HALF
    return pl.pallas_call(
        attend_kernel,
        out_shape=jax.ShapeDtypeStruct((CANDS, HD + EXTRA, HD), dtype),
        in_specs=[pl.BlockSpec(memory_space=pltpu.SMEM)] + [in_vmem] * 3,
        out_specs=in_vmem,
        scratch_shapes=[
            pltpu.VMEM((1, CAND_LANES), jnp.float32),
            pltpu.VMEM((HD, CAND_LANES), jnp.float32),
            pltpu.VMEM((8, CAND_LANES), jnp.float32),
        ],
        compiler_params=pltpu.CompilerParams(vmem_limit_bytes=40 * 2**20),
        cost_estimate=pl.CostEstimate(
            flops=4 * work * HD, bytes_accessed=6 * 2**20, transcendentals=work
        ),
        name="attend",
    )(info, q, k, v)


def merge(a, b):
    in_vmem = pl.BlockSpec(memory_space=pltpu.VMEM)
    return pl.pallas_call(
        merge_kernel,
        out_shape=jax.ShapeDtypeStruct(a.shape, jnp.bfloat16),
        in_specs=[in_vmem] * 2,
        out_specs=in_vmem,
        compiler_params=pltpu.CompilerParams(vmem_limit_bytes=8 * 2**20),
        cost_estimate=pl.CostEstimate(
            flops=8 * a.size, bytes_accessed=6 * a.size, transcendentals=0
        ),
        name="merge",
    )(a, b)


def combine(x):
    in_vmem = pl.BlockSpec(memory_space=pltpu.VMEM)
    return pl.pallas_call(
        combine_kernel,
        out_shape=jax.ShapeDtypeStruct((HD // QPK, QPK * HD), jnp.bfloat16),
        in_specs=[in_vmem],
        out_specs=in_vmem,
        scratch_shapes=[pltpu.VMEM((HD, HD), jnp.float32)],
        compiler_params=pltpu.CompilerParams(vmem_limit_bytes=8 * 2**20),
        cost_estimate=pl.CostEstimate(
            flops=4 * x.size, bytes_accessed=2 * x.size, transcendentals=0
        ),
        name="combine",
    )(x)


def body(queries, keys, values, doc_len):
    swap = [(0, 1), (1, 0)]
    k = jnp.concatenate([keys, lax.ppermute(keys, "c", swap)], axis=0)
    v = jnp.concatenate([values, lax.ppermute(values, "c", swap)], axis=0)

    heads = lax.axis_size(("h", "x"))
    spans = lax.axis_size(("z", "y"))
    blocks = build_blocks(queries, heads, spans)
    q = lax.all_to_all(
        blocks.reshape((spans * heads,) + blocks.shape[2:]), ("z", "y", "h", "x"), 0, 0
    ).reshape(CANDS, spans // CANDS, CAND_LANES, HD)

    chip = lax.axis_index(("z", "y")) * (2 * HALF)
    core, side = lax.axis_index("c"), lax.axis_index("y")
    bases = [chip + core * HALF, chip + (1 - core) * HALF]

    def info(part):
        return jnp.concatenate([doc_len, jnp.stack(bases + [part]).astype(jnp.int32)])

    foreign = attend(info(1 - side), q, k, v, jnp.bfloat16)
    received = lax.ppermute(foreign, "y", swap)
    own = attend(info(side), q, k, v, jnp.float32)
    return combine(lax.all_to_all(merge(own, received), "z", 0, 0))


def solution(mesh):
    fine = Mesh(mesh.devices.reshape(8, 2, 2, 2, 4), ("z", "y", "c", "h", "x"))
    ctx, head = ("z", "y", "c"), ("h", "x")
    placed = (P(ctx + head, None), P(ctx, head), P(ctx, head), P())
    return jax.shard_map(
        body, mesh=fine, in_specs=placed, out_specs=P(ctx, head), check_vma=False
    )
```

```python
import functools

import jax
import jax.numpy as jnp
from jax import lax
from jax.experimental import pallas as pl
from jax.experimental.pallas import tpu as pltpu
from jax.sharding import Mesh
from jax.sharding import PartitionSpec as P

HD = 128
QPK = 8
CANDS = 8
HALF = 4096
CAND_LANES = 128
LANES = CANDS * CAND_LANES
SAMPLE = 128
EXTRA = 16
NONE = -1e30
HIDDEN = -(2.0**100)
LIMIT = 2.0**60
LOG2_SCALE = 1.4426950408889634 / HD**0.5
NT = (((1,), (1,)), ((), ()))
TN = (((0,), (0,)), ((), ()))


def scores(key_rows, query_rows):
    s = lax.dot_general(key_rows, query_rows, NT, preferred_element_type=jnp.float32)
    return s * LOG2_SCALE


def weighted(value_rows, weights):
    return lax.dot_general(
        value_rows, weights.astype(jnp.bfloat16), TN, preferred_element_type=jnp.float32
    )


def block_kernel(q_ref, out_ref, rows_ref):
    rows, heads = q_ref.shape[0], q_ref.shape[1] // (QPK * HD)
    q = q_ref[...].astype(jnp.float32)
    for g in range(heads):
        for i in range(rows):
            for h in range(QPK):
                at = (g * rows + i) * QPK + h
                cut = slice((g * QPK + h) * HD, (g * QPK + h + 1) * HD)
                rows_ref[at : at + 1, :] = q[i : i + 1, cut]
    blocks = rows_ref[...].astype(jnp.bfloat16).reshape(heads, rows * QPK, HD)
    for j in range(out_ref.shape[0]):
        out_ref[j] = blocks


def attend_kernel(info, q_ref, k_ref, v_ref, out_ref, top_ref, acc_ref, sum_ref):
    base_own, base_other = info[CANDS], info[CANDS + 1]
    base = jnp.minimum(base_own, base_other)
    halves = ((0, base_own), (HALF, base_other))
    lengths = [info[c] for c in range(CANDS)]

    def per_candidate(values, lane):
        result = values[0]
        for c in range(1, CANDS):
            result = jnp.where(lane < c * CAND_LANES, result, values[c])
        return result

    def store(first, count, numerators, total, top):
        extra = split_total(total, top, count * HD)
        for j in range(count):
            cut = slice(j * HD, (j + 1) * HD)
            out_ref[first + j, :HD, :] = numerators[:, cut].astype(out_ref.dtype)
            out_ref[first + j, HD:, :] = extra[:, cut].astype(out_ref.dtype)

    queries = jnp.concatenate([q_ref[c] for c in range(CANDS)], axis=0)

    first = pl.multiple_of(jnp.where(base_own == base, 0, HALF), HALF)
    place = base + lax.broadcasted_iota(jnp.int32, (SAMPLE, LANES), 0)
    seen = per_candidate(lengths, lax.broadcasted_iota(jnp.int32, (1, LANES), 1))
    top = jnp.where(place < seen, scores(k_ref[pl.ds(first, SAMPLE), :], queries), NONE)
    top = jnp.max(top, axis=0, keepdims=True).astype(jnp.bfloat16).astype(jnp.float32)
    point = jnp.where(top > 0.5 * NONE, top, -NONE)

    column = lax.broadcasted_iota(jnp.int32, (1, HD), 1)
    limit = jnp.full((1, HD), 2**30, jnp.int32)
    for c in range(CANDS):
        limit = jnp.where(column == c, lengths[c], limit)
    member = lax.broadcasted_iota(jnp.int32, (LANES, HD), 0) // CAND_LANES
    column = lax.broadcasted_iota(jnp.int32, (LANES, HD), 1)
    veto = jnp.where(member == column, HIDDEN, 0.0).astype(jnp.bfloat16)
    query_rows = jnp.concatenate([queries, veto], axis=1)

    total = jnp.zeros((8, LANES), jnp.float32)
    numerators = jnp.zeros((HD, LANES), jnp.float32)
    for half, start in halves:
        lead = (start + 1 - limit).astype(jnp.float32)
        row = lax.broadcasted_iota(jnp.int32, (HALF, HD), 0).astype(jnp.float32)
        beyond = jnp.maximum(row + lead, 0.0).astype(jnp.bfloat16)
        key_rows = jnp.concatenate([k_ref[half : half + HALF, :], beyond], axis=1)
        weights = jnp.exp2(scores(key_rows, query_rows) - point)
        total += jnp.sum(weights.reshape(HALF // 8, 8, LANES), axis=0)
        numerators += weighted(v_ref[half : half + HALF, :], weights)
    total = jnp.sum(total, axis=0, keepdims=True)
    store(0, CANDS, numerators, total, top)

    @pl.when(jnp.logical_not(jnp.max(total) < LIMIT))
    def _():
        block = 512

        @pl.loop(0, CANDS)
        def _(c):
            query_rows = q_ref[c]
            acc_ref[...] = jnp.zeros_like(acc_ref)
            sum_ref[...] = jnp.zeros_like(sum_ref)
            top_ref[...] = jnp.full_like(top_ref, NONE)
            for half, start in halves:

                @pl.loop(0, HALF // block)
                def _(i):
                    at = pl.multiple_of(half + i * block, block)
                    place = start + i * block + lax.broadcasted_iota(
                        jnp.int32, (block, CAND_LANES), 0
                    )
                    usable = place < info[c]
                    s = jnp.where(usable, scores(k_ref[pl.ds(at, block), :], query_rows), NONE)
                    old = top_ref[...]
                    new = jnp.maximum(old, jnp.max(s, axis=0, keepdims=True))
                    shrink = jnp.exp2(old - new)
                    weights = jnp.where(usable, jnp.exp2(s - new), 0.0)
                    sum_ref[...] = sum_ref[...] * shrink + jnp.sum(
                        weights.reshape(block // 8, 8, CAND_LANES), axis=0
                    )
                    acc_ref[...] = acc_ref[...] * shrink + weighted(
                        v_ref[pl.ds(at, block), :], weights
                    )
                    top_ref[...] = new

            top = top_ref[...]
            sent = top.astype(jnp.bfloat16).astype(jnp.float32)
            fit = jnp.where(top > 0.5 * NONE, jnp.exp2(top - sent), 1.0)
            total = jnp.sum(sum_ref[...], axis=0, keepdims=True)
            store(c, 1, acc_ref[...] * fit, total * fit, sent)


def split_total(total, top, width):
    total_high = total.astype(jnp.bfloat16).astype(jnp.float32)
    row = lax.broadcasted_iota(jnp.int32, (EXTRA, width), 0)
    extra = jnp.where(row == 0, top, 0.0)
    extra = jnp.where(row == 1, total_high, extra)
    return jnp.where(row == 2, total - total_high, extra).astype(jnp.bfloat16)


def summed(pieces):
    extras = [piece[HD:, :].astype(jnp.float32) for piece in pieces]
    top = functools.reduce(jnp.maximum, [extra[0:1] for extra in extras])
    total = jnp.zeros((1, HD), jnp.float32)
    numerators = jnp.zeros((HD, HD), jnp.float32)
    for piece, extra in zip(pieces, extras, strict=True):
        scale = jnp.exp2(extra[0:1] - top)
        total += scale * (extra[1:2] + extra[2:3])
        numerators += scale * piece[:HD, :].astype(jnp.float32)
    return numerators, total, top


def merge_kernel(a_ref, b_ref, out_ref):
    for i in range(out_ref.shape[0]):
        numerators, total, top = summed([a_ref[i], b_ref[i]])
        out_ref[i, :HD, :] = numerators.astype(jnp.bfloat16)
        out_ref[i, HD:, :] = split_total(total, top, HD)


def combine_kernel(x_ref, out_ref, turned_ref):
    numerators, total, _ = summed([x_ref[i] for i in range(x_ref.shape[0])])
    turned_ref[...] = (numerators / total).T
    for h in range(QPK):
        rows = turned_ref[pl.ds(h, HD // QPK, stride=QPK), :]
        out_ref[:, h * HD : (h + 1) * HD] = rows.astype(jnp.bfloat16)


def build_blocks(queries, heads, spans):
    in_vmem = pl.BlockSpec(memory_space=pltpu.VMEM)
    rows = queries.shape[0] * QPK
    return pl.pallas_call(
        block_kernel,
        out_shape=jax.ShapeDtypeStruct((spans, heads, rows, HD), jnp.bfloat16),
        in_specs=[in_vmem],
        out_specs=in_vmem,
        scratch_shapes=[pltpu.VMEM((heads * rows, HD), jnp.float32)],
        compiler_params=pltpu.CompilerParams(vmem_limit_bytes=8 * 2**20),
        cost_estimate=pl.CostEstimate(
            flops=0, bytes_accessed=2 * spans * queries.size, transcendentals=0
        ),
        name="build_blocks",
    )(queries)


def attend(info, q, k, v, dtype):
    in_vmem = pl.BlockSpec(memory_space=pltpu.VMEM)
    work = q.size // HD * 2 * HALF
    return pl.pallas_call(
        attend_kernel,
        out_shape=jax.ShapeDtypeStruct((CANDS, HD + EXTRA, HD), dtype),
        in_specs=[pl.BlockSpec(memory_space=pltpu.SMEM)] + [in_vmem] * 3,
        out_specs=in_vmem,
        scratch_shapes=[
            pltpu.VMEM((1, CAND_LANES), jnp.float32),
            pltpu.VMEM((HD, CAND_LANES), jnp.float32),
            pltpu.VMEM((8, CAND_LANES), jnp.float32),
        ],
        compiler_params=pltpu.CompilerParams(vmem_limit_bytes=40 * 2**20),
        cost_estimate=pl.CostEstimate(
            flops=4 * work * HD, bytes_accessed=6 * 2**20, transcendentals=work
        ),
        name="attend",
    )(info, q, k, v)


def merge(a, b):
    in_vmem = pl.BlockSpec(memory_space=pltpu.VMEM)
    return pl.pallas_call(
        merge_kernel,
        out_shape=jax.ShapeDtypeStruct(a.shape, jnp.bfloat16),
        in_specs=[in_vmem] * 2,
        out_specs=in_vmem,
        compiler_params=pltpu.CompilerParams(vmem_limit_bytes=8 * 2**20),
        cost_estimate=pl.CostEstimate(
            flops=8 * a.size, bytes_accessed=6 * a.size, transcendentals=0
        ),
        name="merge",
    )(a, b)


def combine(x):
    in_vmem = pl.BlockSpec(memory_space=pltpu.VMEM)
    return pl.pallas_call(
        combine_kernel,
        out_shape=jax.ShapeDtypeStruct((HD // QPK, QPK * HD), jnp.bfloat16),
        in_specs=[in_vmem],
        out_specs=in_vmem,
        scratch_shapes=[pltpu.VMEM((HD, HD), jnp.float32)],
        compiler_params=pltpu.CompilerParams(vmem_limit_bytes=8 * 2**20),
        cost_estimate=pl.CostEstimate(
            flops=4 * x.size, bytes_accessed=2 * x.size, transcendentals=0
        ),
        name="combine",
    )(x)


def body(queries, keys, values, doc_len):
    swap = [(0, 1), (1, 0)]
    k = jnp.concatenate([keys, lax.ppermute(keys, "c", swap)], axis=0)
    v = jnp.concatenate([values, lax.ppermute(values, "c", swap)], axis=0)

    blocks = build_blocks(
        lax.ppermute(queries, "y", swap), lax.axis_size(("h", "x")), lax.axis_size("z")
    )
    q_foreign = lax.all_to_all(
        blocks.reshape((-1,) + blocks.shape[2:]), ("z", "h", "x"), 0, 0
    ).reshape(CANDS, CAND_LANES, HD)
    q_foreign, k, v = lax.optimization_barrier((q_foreign, k, v))
    q_own = lax.ppermute(q_foreign, "y", swap)

    chip = lax.axis_index(("z", "y")) * (2 * HALF)
    core = lax.axis_index("c")
    bases = jnp.stack([chip + core * HALF, chip + (1 - core) * HALF])
    info = jnp.concatenate([doc_len, bases.astype(jnp.int32)])

    foreign = attend(info, q_foreign, k, v, jnp.bfloat16)
    received = lax.ppermute(foreign, "y", swap)
    own = attend(info, q_own, k, v, jnp.float32)
    return combine(lax.all_to_all(merge(own, received), "z", 0, 0))


def solution(mesh):
    fine = Mesh(mesh.devices.reshape(8, 2, 2, 2, 4), ("z", "y", "c", "h", "x"))
    ctx, head = ("z", "y", "c"), ("h", "x")
    placed = (P(ctx + head, None), P(ctx, head), P(ctx, head), P())
    return jax.shard_map(
        body, mesh=fine, in_specs=placed, out_specs=P(ctx, head), check_vma=False
    )
```

```python
import functools

import jax
import jax.numpy as jnp
from jax import lax
from jax.experimental import pallas as pl
from jax.experimental.pallas import tpu as pltpu
from jax.sharding import Mesh
from jax.sharding import PartitionSpec as P

HD = 128
QPK = 8
CANDS = 8
HALF = 4096
CAND_LANES = 128
LANES = CANDS * CAND_LANES
SAMPLE = 128
EXTRA = 16
NONE = -1e30
HIDDEN = -(2.0**100)
LIMIT = 2.0**60
LOG2_SCALE = 1.4426950408889634 / HD**0.5
NT = (((1,), (1,)), ((), ()))
TN = (((0,), (0,)), ((), ()))


def scores(key_rows, query_rows):
    s = lax.dot_general(key_rows, query_rows, NT, preferred_element_type=jnp.float32)
    return s * LOG2_SCALE


def weighted(value_rows, weights):
    return lax.dot_general(
        value_rows, weights.astype(jnp.bfloat16), TN, preferred_element_type=jnp.float32
    )


def block_kernel(q_ref, out_ref, rows_ref):
    rows, heads = q_ref.shape[0], q_ref.shape[1] // (QPK * HD)
    q = q_ref[...].astype(jnp.float32)
    for g in range(heads):
        for i in range(rows):
            for h in range(QPK):
                at = (g * rows + i) * QPK + h
                cut = slice((g * QPK + h) * HD, (g * QPK + h + 1) * HD)
                rows_ref[at : at + 1, :] = q[i : i + 1, cut]
    blocks = rows_ref[...].astype(jnp.bfloat16).reshape(heads, rows * QPK, HD)
    for j in range(out_ref.shape[0]):
        out_ref[j] = blocks


def fetching_kernel(
    info, q_ref, k_ref, v_own, v_other, out_ref, top_ref, acc_ref, sum_ref, v_ref, arrived
):
    copies = [
        pltpu.make_async_copy(v_own, v_ref.at[:HALF], arrived.at[0]),
        pltpu.make_async_copy(v_other, v_ref.at[HALF:], arrived.at[1]),
    ]
    for copy in copies:
        copy.start()
    attend_kernel(info, q_ref, k_ref, v_ref, out_ref, top_ref, acc_ref, sum_ref, copies)


def attend_kernel(
    info, q_ref, k_ref, v_ref, out_ref, top_ref, acc_ref, sum_ref, copies=(None, None)
):
    base_own, base_other = info[CANDS], info[CANDS + 1]
    base = jnp.minimum(base_own, base_other)
    halves = ((0, base_own), (HALF, base_other))
    lengths = [info[c] for c in range(CANDS)]

    def per_candidate(values, lane):
        result = values[0]
        for c in range(1, CANDS):
            result = jnp.where(lane < c * CAND_LANES, result, values[c])
        return result

    def store(first, count, numerators, total, top):
        extra = split_total(total, top, count * HD)
        for j in range(count):
            cut = slice(j * HD, (j + 1) * HD)
            out_ref[first + j, :HD, :] = numerators[:, cut].astype(out_ref.dtype)
            out_ref[first + j, HD:, :] = extra[:, cut].astype(out_ref.dtype)

    queries = jnp.concatenate([q_ref[c] for c in range(CANDS)], axis=0)

    first = pl.multiple_of(jnp.where(base_own == base, 0, HALF), HALF)
    place = base + lax.broadcasted_iota(jnp.int32, (SAMPLE, LANES), 0)
    seen = per_candidate(lengths, lax.broadcasted_iota(jnp.int32, (1, LANES), 1))
    top = jnp.where(place < seen, scores(k_ref[pl.ds(first, SAMPLE), :], queries), NONE)
    top = jnp.max(top, axis=0, keepdims=True).astype(jnp.bfloat16).astype(jnp.float32)
    point = jnp.where(top > 0.5 * NONE, top, -NONE)

    column = lax.broadcasted_iota(jnp.int32, (1, HD), 1)
    limit = jnp.full((1, HD), 2**30, jnp.int32)
    for c in range(CANDS):
        limit = jnp.where(column == c, lengths[c], limit)
    member = lax.broadcasted_iota(jnp.int32, (LANES, HD), 0) // CAND_LANES
    column = lax.broadcasted_iota(jnp.int32, (LANES, HD), 1)
    veto = jnp.where(member == column, HIDDEN, 0.0).astype(jnp.bfloat16)
    query_rows = jnp.concatenate([queries, veto], axis=1)

    total = jnp.zeros((8, LANES), jnp.float32)
    numerators = jnp.zeros((HD, LANES), jnp.float32)
    for copy, (half, start) in zip(copies, halves, strict=True):
        if copy is not None:
            copy.wait()
        lead = (start + 1 - limit).astype(jnp.float32)
        row = lax.broadcasted_iota(jnp.int32, (HALF, HD), 0).astype(jnp.float32)
        beyond = jnp.maximum(row + lead, 0.0).astype(jnp.bfloat16)
        key_rows = jnp.concatenate([k_ref[half : half + HALF, :], beyond], axis=1)
        weights = jnp.exp2(scores(key_rows, query_rows) - point)
        total += jnp.sum(weights.reshape(HALF // 8, 8, LANES), axis=0)
        numerators += weighted(v_ref[half : half + HALF, :], weights)
    total = jnp.sum(total, axis=0, keepdims=True)
    store(0, CANDS, numerators, total, top)

    @pl.when(jnp.logical_not(jnp.max(total) < LIMIT))
    def _():
        block = 512

        @pl.loop(0, CANDS)
        def _(c):
            query_rows = q_ref[c]
            acc_ref[...] = jnp.zeros_like(acc_ref)
            sum_ref[...] = jnp.zeros_like(sum_ref)
            top_ref[...] = jnp.full_like(top_ref, NONE)
            for half, start in halves:

                @pl.loop(0, HALF // block)
                def _(i):
                    at = pl.multiple_of(half + i * block, block)
                    place = start + i * block + lax.broadcasted_iota(
                        jnp.int32, (block, CAND_LANES), 0
                    )
                    usable = place < info[c]
                    s = jnp.where(usable, scores(k_ref[pl.ds(at, block), :], query_rows), NONE)
                    old = top_ref[...]
                    new = jnp.maximum(old, jnp.max(s, axis=0, keepdims=True))
                    shrink = jnp.exp2(old - new)
                    weights = jnp.where(usable, jnp.exp2(s - new), 0.0)
                    sum_ref[...] = sum_ref[...] * shrink + jnp.sum(
                        weights.reshape(block // 8, 8, CAND_LANES), axis=0
                    )
                    acc_ref[...] = acc_ref[...] * shrink + weighted(
                        v_ref[pl.ds(at, block), :], weights
                    )
                    top_ref[...] = new

            top = top_ref[...]
            sent = top.astype(jnp.bfloat16).astype(jnp.float32)
            fit = jnp.where(top > 0.5 * NONE, jnp.exp2(top - sent), 1.0)
            total = jnp.sum(sum_ref[...], axis=0, keepdims=True)
            store(c, 1, acc_ref[...] * fit, total * fit, sent)


def split_total(total, top, width):
    total_high = total.astype(jnp.bfloat16).astype(jnp.float32)
    row = lax.broadcasted_iota(jnp.int32, (EXTRA, width), 0)
    extra = jnp.where(row == 0, top, 0.0)
    extra = jnp.where(row == 1, total_high, extra)
    return jnp.where(row == 2, total - total_high, extra).astype(jnp.bfloat16)


def summed(pieces):
    extras = [piece[HD:, :].astype(jnp.float32) for piece in pieces]
    top = functools.reduce(jnp.maximum, [extra[0:1] for extra in extras])
    total = jnp.zeros((1, HD), jnp.float32)
    numerators = jnp.zeros((HD, HD), jnp.float32)
    for piece, extra in zip(pieces, extras, strict=True):
        scale = jnp.exp2(extra[0:1] - top)
        total += scale * (extra[1:2] + extra[2:3])
        numerators += scale * piece[:HD, :].astype(jnp.float32)
    return numerators, total, top


def merge_kernel(a_ref, b_ref, out_ref):
    for i in range(out_ref.shape[0]):
        numerators, total, top = summed([a_ref[i], b_ref[i]])
        out_ref[i, :HD, :] = numerators.astype(jnp.bfloat16)
        out_ref[i, HD:, :] = split_total(total, top, HD)


def combine_kernel(x_ref, out_ref, turned_ref):
    numerators, total, _ = summed([x_ref[i] for i in range(x_ref.shape[0])])
    turned_ref[...] = (numerators / total).T
    for h in range(QPK):
        rows = turned_ref[pl.ds(h, HD // QPK, stride=QPK), :]
        out_ref[:, h * HD : (h + 1) * HD] = rows.astype(jnp.bfloat16)


def build_blocks(queries, heads, spans):
    in_vmem = pl.BlockSpec(memory_space=pltpu.VMEM)
    rows = queries.shape[0] * QPK
    return pl.pallas_call(
        block_kernel,
        out_shape=jax.ShapeDtypeStruct((spans, heads, rows, HD), jnp.bfloat16),
        in_specs=[in_vmem],
        out_specs=in_vmem,
        scratch_shapes=[pltpu.VMEM((heads * rows, HD), jnp.float32)],
        compiler_params=pltpu.CompilerParams(vmem_limit_bytes=8 * 2**20),
        cost_estimate=pl.CostEstimate(
            flops=0, bytes_accessed=2 * spans * queries.size, transcendentals=0
        ),
        name="build_blocks",
    )(queries)


def attend(info, q, k, values, dtype):
    in_vmem = pl.BlockSpec(memory_space=pltpu.VMEM)
    work = q.size // HD * 2 * HALF
    kernel, value_specs, extra_scratch = attend_kernel, [in_vmem], []
    if len(values) == 2:
        kernel = fetching_kernel
        value_specs = [pl.BlockSpec(memory_space=pltpu.HBM)] * 2
        extra_scratch = [
            pltpu.VMEM((2 * HALF, HD), jnp.bfloat16),
            pltpu.SemaphoreType.DMA((2,)),
        ]
    return pl.pallas_call(
        kernel,
        out_shape=jax.ShapeDtypeStruct((CANDS, HD + EXTRA, HD), dtype),
        in_specs=[pl.BlockSpec(memory_space=pltpu.SMEM)] + [in_vmem] * 2 + value_specs,
        out_specs=in_vmem,
        scratch_shapes=[
            pltpu.VMEM((1, CAND_LANES), jnp.float32),
            pltpu.VMEM((HD, CAND_LANES), jnp.float32),
            pltpu.VMEM((8, CAND_LANES), jnp.float32),
        ]
        + extra_scratch,
        compiler_params=pltpu.CompilerParams(vmem_limit_bytes=40 * 2**20),
        cost_estimate=pl.CostEstimate(
            flops=4 * work * HD, bytes_accessed=6 * 2**20, transcendentals=work
        ),
        name="attend",
    )(info, q, k, *values)


def merge(a, b):
    in_vmem = pl.BlockSpec(memory_space=pltpu.VMEM)
    return pl.pallas_call(
        merge_kernel,
        out_shape=jax.ShapeDtypeStruct(a.shape, jnp.bfloat16),
        in_specs=[in_vmem] * 2,
        out_specs=in_vmem,
        compiler_params=pltpu.CompilerParams(vmem_limit_bytes=8 * 2**20),
        cost_estimate=pl.CostEstimate(
            flops=8 * a.size, bytes_accessed=6 * a.size, transcendentals=0
        ),
        name="merge",
    )(a, b)


def combine(x):
    in_vmem = pl.BlockSpec(memory_space=pltpu.VMEM)
    return pl.pallas_call(
        combine_kernel,
        out_shape=jax.ShapeDtypeStruct((HD // QPK, QPK * HD), jnp.bfloat16),
        in_specs=[in_vmem],
        out_specs=in_vmem,
        scratch_shapes=[pltpu.VMEM((HD, HD), jnp.float32)],
        compiler_params=pltpu.CompilerParams(vmem_limit_bytes=8 * 2**20),
        cost_estimate=pl.CostEstimate(
            flops=4 * x.size, bytes_accessed=2 * x.size, transcendentals=0
        ),
        name="combine",
    )(x)


def body(queries, keys, values, doc_len):
    swap = [(0, 1), (1, 0)]
    k = jnp.concatenate([keys, lax.ppermute(keys, "c", swap)], axis=0)
    v_other = lax.ppermute(values, "c", swap)
    v = jnp.concatenate([values, v_other], axis=0)

    blocks = build_blocks(
        lax.ppermute(queries, "y", swap), lax.axis_size(("h", "x")), lax.axis_size("z")
    )
    q_foreign = lax.all_to_all(
        blocks.reshape((-1,) + blocks.shape[2:]), ("z", "h", "x"), 0, 0
    ).reshape(CANDS, CAND_LANES, HD)
    q_foreign, k, v = lax.optimization_barrier((q_foreign, k, v))
    q_own = lax.ppermute(q_foreign, "y", swap)

    chip = lax.axis_index(("z", "y")) * (2 * HALF)
    core = lax.axis_index("c")
    bases = jnp.stack([chip + core * HALF, chip + (1 - core) * HALF])
    info = jnp.concatenate([doc_len, bases.astype(jnp.int32)])

    foreign = attend(info, q_foreign, k, (values, v_other), jnp.bfloat16)
    received = lax.ppermute(foreign, "y", swap)
    own = attend(info, q_own, k, (v,), jnp.float32)
    return combine(lax.all_to_all(merge(own, received), "z", 0, 0))


def solution(mesh):
    fine = Mesh(mesh.devices.reshape(8, 2, 2, 2, 4), ("z", "y", "c", "h", "x"))
    ctx, head = ("z", "y", "c"), ("h", "x")
    placed = (P(ctx + head, None), P(ctx, head), P(ctx, head), P())
    return jax.shard_map(
        body, mesh=fine, in_specs=placed, out_specs=P(ctx, head), check_vma=False
    )
```
